32 devices in a mesh: groups: 2 (over x), row: 16 (over z, y, core).
Axes of the slice: x: 2, y: 2, z: 4, core: 2. Of those that a mesh axis runs over, the one named last changes fastest.
Arguments:
- features: bfloat16 [64, 32, 4, 256], P('groups', 'row'), parts along dimension 0, may hold values from -6 to 6
- axial_taps: float32 [31, 256], replicated, may hold values from -1 to 1
- radial_taps: float32 [31, 256], replicated, may hold values from -1 to 1
- conv_bias: float32 [256], replicated, may hold values from -6 to 6
- ln_gain: float32 [256], replicated, may hold values from 0.5 to 1.5
- ln_bias: float32 [256], replicated, may hold values from -3 to 3
- w_in: bfloat16 [1024, 256], P('row'), may hold values from -0.375 to 0.375
- b_in: bfloat16 [1024], P('row'), may hold values from -3 to 3
- w_out: bfloat16 [1024, 256], P('row'), may hold values from -0.1875 to 0.1875
- b_out: float32 [256], replicated, may hold values from -1.75 to 1.75
- layer_scale: float32 [256], replicated, may hold values from 0.5 to 2
Outputs:
- block_out: bfloat16 [64, 32, 4, 256], P('groups', 'row'), parts along dimension 0
The draws below stay inside these ranges and needn't reach their ends.
There are 2 independent parts, one for each index of `groups`. The reference program is written for one: setup_inputs(seed, part) draws one part's arguments, and reference() takes and returns one part's arrays. A program takes and returns all parts, laid end to end along the dimension named above; an argument that names none is the same for every part. Nothing has to cross between parts.
All inputs are finite; a program needn't handle non-finite values.
Results may differ from the reference program's by a relative error of at most 0.01.
Values may be sent and summed in bfloat16 or wider, within the bound.
A program may use at most 64 MiB of HBM per device.

```python
import math
from functools import partial
import jax
import jax.numpy as jnp
from jax import lax

C = 256
HID = 1024
TAPS = 31
AX_DEV = 2
THETA = 4
AXIAL = 32
RADIAL = 32


def shard_levels(key, shape, pieces, least, largest):
    loudness = 1.0
    for axis_at, parts in pieces:
        draws = jax.random.uniform(jax.random.fold_in(jax.random.fold_in(key, 6), axis_at), (parts,), jnp.float32, least / len(pieces), largest / len(pieces))
        loudness = loudness * jnp.repeat(jnp.exp(draws), shape[axis_at] // parts).reshape((-1,) + (1,) * (len(shape) - 1 - axis_at))
    return loudness


def normal_values(rng, dims, width, reach, pieces=(), dtype=jnp.bfloat16):
    level = shard_levels(rng, dims, pieces, -0.22, 0.18) if pieces else 1.0
    entries = jax.random.normal(rng, dims, jnp.float32) * width * level
    return jnp.minimum(jnp.maximum(entries, -reach), reach).astype(dtype)


def setup_inputs(seed: int = 0, part: int = 0) -> dict:
    key_of = jax.random.split(jax.random.key(seed), 12)
    part_splits = jax.random.split(jax.random.fold_in(key_of[11], part), 12)
    features = normal_values(part_splits[0], (AXIAL, RADIAL, THETA, C), 1.0, 6.0, ((1, 16),))
    axial_taps = normal_values(key_of[1], (TAPS, C), TAPS ** -0.5, 1.0, (), jnp.float32)
    radial_taps = normal_values(key_of[2], (TAPS, C), TAPS ** -0.5, 1.0, (), jnp.float32)
    conv_bias = normal_values(key_of[3], (C,), 1.0, 6.0, (), jnp.float32)
    ln_gain = jnp.clip(jax.random.uniform(key_of[4], (C,), jnp.float32, 0.5, 1.5), 0.5, 1.5)
    ln_bias = normal_values(key_of[5], (C,), 0.5, 3.0, (), jnp.float32)
    w_in = normal_values(key_of[6], (HID, C), C ** -0.5, 0.375, ((0, 16),))
    b_in = normal_values(key_of[7], (HID,), 0.5, 3.0, ((0, 16),))
    w_out = normal_values(key_of[8], (HID, C), HID ** -0.5, 0.1875, ((0, 16),))
    b_out = normal_values(key_of[9], (C,), 0.3, 1.75, (), jnp.float32)
    layer_scale = jnp.clip(jnp.exp(jax.random.uniform(key_of[10], (C,), jnp.float32, math.log(0.5), math.log(2.0))), 0.5, 2.0)
    return {"features": features, "axial_taps": axial_taps, "radial_taps": radial_taps, "conv_bias": conv_bias, "ln_gain": ln_gain, "ln_bias": ln_bias, "w_in": w_in, "b_in": b_in, "w_out": w_out, "b_out": b_out, "layer_scale": layer_scale}


def shifted_sum(source, tap_table, along_dim):
    half_span = tap_table.shape[0] // 2
    pad_widths = [(0, 0)] * source.ndim
    pad_widths[along_dim] = (half_span, half_span)
    padded = jnp.pad(source, pad_widths)
    extent = source.shape[along_dim]
    total_sum = jnp.zeros(source.shape, jnp.float32)
    for offset in range(tap_table.shape[0]):
        window = lax.slice_in_dim(padded, offset, offset + extent, axis=along_dim)
        total_sum = total_sum + window.astype(jnp.float32) * tap_table[offset]
    return total_sum

def block_mlp(params, row_block):
    w_in, b_in, w_out, ln_gain, ln_bias, b_out, layer_scale = params
    values = row_block.astype(jnp.float32)
    average = lax.optimization_barrier(jnp.mean(values, axis=-1, keepdims=True))
    centred = values - average
    variance = lax.optimization_barrier(jnp.mean(centred * centred, axis=-1, keepdims=True))
    normed = (centred * lax.rsqrt(variance + 1e-06) * ln_gain + ln_bias).astype(jnp.bfloat16)
    pre_act = lax.dot_general(normed, w_in, (((1,), (1,)), ((), ())), preferred_element_type=jnp.float32)
    pre_act = pre_act + b_in.astype(jnp.float32)
    hidden = jax.nn.gelu(pre_act, approximate=True).astype(jnp.bfloat16)
    projected = jnp.dot(hidden, w_out, preferred_element_type=jnp.float32) + b_out
    return (layer_scale * projected).astype(jnp.bfloat16)

def reference(features, axial_taps, radial_taps, conv_bias, ln_gain, ln_bias, w_in, b_in, w_out, b_out, layer_scale):
    params = (w_in, b_in, w_out, ln_gain, ln_bias, b_out, layer_scale)
    planes = jnp.moveaxis(features, 2, 0)
    channels = features.shape[-1]

    def one_plane(theta_plane):
        axial_mixed = shifted_sum(theta_plane, axial_taps, 0).astype(jnp.bfloat16)
        radial_mixed = (shifted_sum(axial_mixed, radial_taps, 1) + conv_bias).astype(jnp.bfloat16)
        groups = radial_mixed.reshape(AXIAL // AX_DEV, AX_DEV * RADIAL, channels)
        branch = lax.map(partial(block_mlp, params), groups).reshape(AXIAL, RADIAL, channels)
        return (theta_plane.astype(jnp.float32) + branch.astype(jnp.float32)).astype(jnp.bfloat16)
    result = lax.map(one_plane, planes)
    return jnp.moveaxis(result, 0, 2)
```

```python
import functools

import jax
import jax.numpy as jnp
from jax import lax
from jax.experimental import pallas as pl
from jax.experimental.pallas import tpu as pltpu
from jax.sharding import PartitionSpec as P

MESH_ID = pl.DeviceIdType.MESH
F32 = jnp.float32
BF16 = jnp.bfloat16


def kernel(
    n, taps, al, hl,
    x_ref, at_ref, rt_ref, cb_ref, lg_ref, lb_ref, wi_ref, bi_ref, wo_ref, bo_ref, ls_ref,
    o_ref,
    xpad, even, odd, send1, recv1, send2, recv2, wts, normed,
    s1_sem, r1_sem, s2_sem, r2_sem, ws_sem, wr_sem,
):
    channels = x_ref.shape[1]
    axial = x_ref.shape[0] // 8
    half = taps // 2
    per = channels // hl
    chips = n // 2
    me = lax.axis_index("row")
    grp = lax.axis_index("groups")
    core = lax.rem(me, 2)
    my_chip = lax.div(me, 2)
    sibling = me + 1 - 2 * core
    my_slot = core * chips + my_chip
    base = core * chips
    other = (1 - core) * chips

    def to(d):
        return (grp, d)

    def ring(i, size, start):
        d = start + i
        return jnp.where(d >= size, d - size, d)

    barrier = pltpu.get_barrier_semaphore()

    def greet(i, c):
        pl.semaphore_signal(barrier, inc=1, device_id=to(ring(i, n, me)), device_id_type=MESH_ID)
        return c

    lax.fori_loop(1, n, greet, 0)

    wts[my_slot, 0:hl, :] = wi_ref[...]
    wts[my_slot, hl : 2 * hl, :] = wo_ref[...]
    unit = lax.broadcasted_iota(jnp.int32, (hl, channels), 0)
    lane = lax.broadcasted_iota(jnp.int32, (hl, channels), 1)
    place = (lane == unit + lax.rem(my_slot, per) * hl).astype(F32).astype(BF16)
    bias16 = jnp.broadcast_to(bi_ref[...].astype(F32), (16, hl)).astype(BF16)
    wts[my_slot, 2 * hl : 2 * hl + 16, :] = jnp.dot(
        bias16, place, preferred_element_type=F32
    ).astype(BF16)

    xpad[0:half] = jnp.zeros((half, 8, channels), F32)
    xpad[axial + half : axial + 2 * half] = jnp.zeros((half, 8, channels), F32)
    zeros8 = jnp.zeros((8, al, 8, channels), F32)
    even[0:8] = zeros8
    even[n + 8 : n + 16] = zeros8
    odd[0:8] = zeros8
    odd[n + 7 : n + 15] = zeros8
    odd[n + 15] = zeros8[0]

    def widen(i, c):
        rows = x_ref[pl.ds(pl.multiple_of(i * 64, 64), 64), :].astype(F32)
        xpad[pl.ds(half + i * 8, 8)] = rows.reshape(8, 8, channels)
        return c

    lax.fori_loop(0, axial // 8, widen, 0)

    def axial_chunk(i, c):
        acc = jnp.zeros((8, 8, channels), F32)
        for k in range(taps):
            acc = acc + xpad[pl.ds(i * 8 + k, 8)] * at_ref[k : k + 1, :][None]
        send1[pl.ds(i * 4, 4)] = acc.reshape(4, 16, channels).astype(BF16)
        return c

    lax.fori_loop(0, axial // 8, axial_chunk, 0)

    pl.semaphore_wait(barrier, n - 1)

    def exchange1(i, c):
        d = ring(i, n, me)
        pltpu.make_async_remote_copy(
            src_ref=send1.at[d], dst_ref=recv1.at[me], send_sem=s1_sem, recv_sem=r1_sem,
            device_id=to(d), device_id_type=MESH_ID,
        ).start()
        return c

    lax.fori_loop(1, n, exchange1, 0)

    def weight_copy(slot, d):
        return pltpu.make_async_remote_copy(
            src_ref=wts.at[slot], dst_ref=wts.at[slot], send_sem=ws_sem, recv_sem=wr_sem.at[slot],
            device_id=to(d), device_id_type=MESH_ID,
        )

    weight_copy(my_slot, sibling).start()

    def gather(i, c):
        weight_copy(my_slot, 2 * ring(i, chips, my_chip) + core).start()
        return c

    lax.fori_loop(1, chips, gather, 0)

    recv1[me] = send1[me]
    arrived = recv1.at[pl.ds(0, n - 1)]
    pltpu.make_async_copy(arrived, arrived, r1_sem).wait()

    def pairs(s, c):
        v = recv1[s].astype(F32).reshape(al, 8, channels)
        even[s + 8] = v
        for a in range(al):
            odd[s + 8, a, 0:4, :] = v[a, 4:8]
            odd[s + 7, a, 4:8, :] = v[a, 0:4]
        return c

    lax.fori_loop(0, n, pairs, 0)

    def radial_chunk(i, c):
        p = i * 4
        acc = jnp.zeros((4, al, 8, channels), F32)
        for k in range(taps):
            shift = k - half
            if shift % 2 == 0:
                window = even[pl.ds(p + 8 + shift // 2, 4)]
            else:
                window = odd[pl.ds(p + 8 + (shift - 1) // 2, 4)]
            acc = acc + window * rt_ref[k : k + 1, :][None, None]
        acc = acc + cb_ref[...][None, None]
        send2[pl.ds(p, 4)] = acc.reshape(4, al * 8, channels).astype(BF16)
        return c

    lax.fori_loop(0, n // 4, radial_chunk, 0)

    def exchange2(i, c):
        d = ring(i, n, me)
        pltpu.make_async_remote_copy(
            src_ref=send2.at[d], dst_ref=recv2.at[me], send_sem=s2_sem, recv_sem=r2_sem,
            device_id=to(d), device_id_type=MESH_ID,
        ).start()
        return c

    lax.fori_loop(1, n, exchange2, 0)
    recv2[me] = send2[me]

    def forward(i, c):
        slot = base + ring(chips - i, chips, my_chip)
        weight_copy(slot, sibling).wait_recv()
        weight_copy(slot, sibling).start()
        return c

    lax.fori_loop(1, chips, forward, 0)

    arrived2 = recv2.at[pl.ds(0, n - 1)]
    pltpu.make_async_copy(arrived2, arrived2, r2_sem).wait()

    block = min(16, n)
    rows = block * 16

    def norm(b, c):
        v = recv2[pl.ds(b * block, block)].reshape(rows, channels).astype(F32)
        average = jnp.mean(v, axis=-1, keepdims=True)
        centred = v - average
        variance = jnp.mean(centred * centred, axis=-1, keepdims=True)
        z = centred * lax.rsqrt(variance + 1e-06) * lg_ref[...] + lb_ref[...]
        normed[pl.ds(pl.multiple_of(b * rows, rows), rows), :] = z.astype(BF16)
        return c

    lax.fori_loop(0, n // block, norm, 0)

    def flat(w):
        if hl % 16:
            return w.astype(F32).reshape(per * hl, channels).astype(BF16)
        return w.reshape(per * hl, channels)

    def project(z, first):
        w_in = flat(wts[pl.ds(first, per), 0:hl, :])
        w_out = flat(wts[pl.ds(first, per), hl : 2 * hl, :])
        b_in = jnp.sum(wts[pl.ds(first, per), 2 * hl : 2 * hl + 16, :].astype(F32), axis=0)[0:1]
        u = lax.dot_general(z, w_in, (((1,), (1,)), ((), ())), preferred_element_type=F32) + b_in
        g = 0.5 * u * (1.0 + jnp.tanh(0.7978845608028654 * (u + 0.044715 * (u * u * u))))
        return jnp.dot(g.astype(BF16), w_out, preferred_element_type=F32)

    def others(i, c):
        weight_copy(other + i, sibling).wait_recv()
        return c

    def mlp(b, c, late):
        at = pl.ds(pl.multiple_of(b * rows, rows), rows)
        z = normed[at, :]
        total = project(z, base)
        for g in range(1, chips // per):
            total = total + project(z, base + g * per)
        if late:
            lax.fori_loop(0, chips, others, 0)
        for g in range(chips // per):
            total = total + project(z, other + g * per)
        branch = (ls_ref[...] * (total + bo_ref[...])).astype(BF16)
        o_ref[at, :] = (x_ref[at, :].astype(F32) + branch.astype(F32)).astype(BF16)
        return c

    mlp(0, 0, True)
    if n // block > 1:
        lax.fori_loop(1, n // block, lambda b, c: mlp(b, c, False), 0)

    sent = send1.at[pl.ds(0, n - 1)]
    pltpu.make_async_copy(sent, sent, s1_sem).wait()
    sent2 = send2.at[pl.ds(0, n - 1)]
    pltpu.make_async_copy(sent2, sent2, s2_sem).wait()
    passed = wts.at[pl.ds(0, n - 1)]
    pltpu.make_async_copy(passed, passed, ws_sem).wait()


def local(
    features,
    axial_taps,
    radial_taps,
    conv_bias,
    ln_gain,
    ln_bias,
    w_in,
    b_in,
    w_out,
    b_out,
    layer_scale,
    n,
):
    axial, radial, theta, channels = features.shape
    taps = axial_taps.shape[0]
    hl = w_in.shape[0]
    al = axial // n
    assert radial * theta == 8 and al == 2 and channels == 256 and taps == 31
    flat = features.reshape(axial * 8, channels)

    def row(v):
        return v.reshape(1, -1)

    vmem = pl.BlockSpec(memory_space=pltpu.VMEM)
    dma = pltpu.SemaphoreType.DMA
    out = pl.pallas_call(
        functools.partial(kernel, n, taps, al, hl),
        out_shape=jax.ShapeDtypeStruct(flat.shape, BF16),
        in_specs=[vmem] * 11,
        out_specs=vmem,
        scratch_shapes=[
            pltpu.VMEM((axial + taps - 1, 8, channels), F32),
            pltpu.VMEM((n + 16, al, 8, channels), F32),
            pltpu.VMEM((n + 16, al, 8, channels), F32),
            pltpu.VMEM((n, 16, channels), BF16),
            pltpu.VMEM((n, 16, channels), BF16),
            pltpu.VMEM((n, 16, channels), BF16),
            pltpu.VMEM((n, 16, channels), BF16),
            pltpu.VMEM((n, 2 * hl + 16, channels), BF16),
            pltpu.VMEM((axial * 8, channels), BF16),
            dma, dma, dma, dma, dma,
            dma((n,)),
        ],
        compiler_params=pltpu.CompilerParams(
            collective_id=0, has_side_effects=True, vmem_limit_bytes=40 * 1024 * 1024
        ),
        cost_estimate=pl.CostEstimate(
            flops=axial * 8 * channels * 4 * (n * hl + taps),
            bytes_accessed=4 * axial * 8 * channels + 4 * n * hl * channels,
            transcendentals=axial * 8 * n * hl,
        ),
    )(
        flat, axial_taps, radial_taps, row(conv_bias), row(ln_gain), row(ln_bias),
        w_in, row(b_in), w_out, row(b_out), row(layer_scale),
    )
    return out.reshape(features.shape)


def solution(mesh):
    in_specs = (
        P("groups", "row", None, None),
        P(),
        P(),
        P(),
        P(),
        P(),
        P("row", None),
        P("row"),
        P("row", None),
        P(),
        P(),
    )
    out_specs = P("groups", "row", None, None)
    body = functools.partial(local, n=mesh.shape["row"])
    return jax.shard_map(body, mesh=mesh, in_specs=in_specs, out_specs=out_specs, check_vma=False)
```

```python
import functools

import jax
import jax.numpy as jnp
from jax import lax
from jax.experimental import pallas as pl
from jax.experimental.pallas import tpu as pltpu
from jax.sharding import PartitionSpec as P

MESH_ID = pl.DeviceIdType.MESH
F32 = jnp.float32
BF16 = jnp.bfloat16


def kernel(
    n, inner, taps, al, hl,
    x_ref, at_ref, rt_ref, cb_ref, lg_ref, lb_ref, wi_ref, bi_ref, wo_ref, bo_ref, ls_ref,
    o_ref,
    xpad, even, odd, send1, recv1, send2, recv2, wts, bias, normed,
    s1_sem, r1_sem, s2_sem, r2_sem, ws_sem, bs_sem, br_sem, wr_sem,
):
    channels = x_ref.shape[1]
    axial = x_ref.shape[0] // 8
    half = taps // 2
    per = channels // hl
    chips = n // 2
    me = lax.axis_index("row")
    grp = lax.axis_index("groups")
    core = lax.rem(me, 2)
    my_chip = lax.div(me, 2)
    sibling = me + 1 - 2 * core
    my_slot = core * chips + my_chip
    base = core * chips
    other = (1 - core) * chips
    outer = chips // inner
    my_z = lax.div(my_chip, inner)
    my_y = lax.rem(my_chip, inner)

    def to(d):
        return (grp, d)

    def ring(i, size, start):
        d = start + i
        return jnp.where(d >= size, d - size, d)

    barrier = pltpu.get_barrier_semaphore()

    def greet(i, c):
        pl.semaphore_signal(barrier, inc=1, device_id=to(ring(i, n, me)), device_id_type=MESH_ID)
        return c

    lax.fori_loop(1, n, greet, 0)
    pl.semaphore_signal(barrier, inc=1, device_id=(1 - grp, me), device_id_type=MESH_ID)

    wts[my_slot] = wi_ref[...]
    wts[n + my_slot] = wo_ref[...]
    unit = lax.broadcasted_iota(jnp.int32, (hl, channels), 0)
    lane = lax.broadcasted_iota(jnp.int32, (hl, channels), 1)
    place = (lane == unit + lax.rem(my_slot, per) * hl).astype(F32).astype(BF16)
    bias16 = jnp.broadcast_to(bi_ref[...].astype(F32), (16, hl)).astype(BF16)
    bias[my_slot] = jnp.dot(bias16, place, preferred_element_type=F32)[0:1]

    xpad[0:half] = jnp.zeros((half, 8, channels), F32)
    xpad[axial + half : axial + 2 * half] = jnp.zeros((half, 8, channels), F32)
    zeros8 = jnp.zeros((8, al, 8, channels), F32)
    even[0:8] = zeros8
    even[n + 8 : n + 16] = zeros8
    odd[0:8] = zeros8
    odd[n + 7 : n + 15] = zeros8
    odd[n + 15] = zeros8[0]

    def widen(i, c):
        rows = x_ref[pl.ds(pl.multiple_of(i * 64, 64), 64), :].astype(F32)
        xpad[pl.ds(half + i * 8, 8)] = rows.reshape(8, 8, channels)
        return c

    lax.fori_loop(0, axial // 8, widen, 0)

    def axial_chunk(i, c):
        acc = jnp.zeros((8, 8, channels), F32)
        for k in range(taps):
            acc = acc + xpad[pl.ds(i * 8 + k, 8)] * at_ref[k : k + 1, :][None]
        send1[pl.ds(i * 4, 4)] = acc.reshape(4, 16, channels).astype(BF16)
        return c

    lax.fori_loop(0, axial // 8, axial_chunk, 0)

    pl.semaphore_wait(barrier, n)

    def exchange1(i, c):
        d = ring(i, n, me)
        pltpu.make_async_remote_copy(
            src_ref=send1.at[d], dst_ref=recv1.at[me], send_sem=s1_sem, recv_sem=r1_sem,
            device_id=to(d), device_id_type=MESH_ID,
        ).start()
        return c

    lax.fori_loop(1, n, exchange1, 0)

    mine = grp * n
    theirs = (1 - grp) * n

    def piece_copy(piece, g, d):
        return pltpu.make_async_remote_copy(
            src_ref=wts.at[piece], dst_ref=wts.at[piece], send_sem=ws_sem,
            recv_sem=wr_sem.at[piece], device_id=(g, d), device_id_type=MESH_ID,
        )

    def chip_of(z, y):
        return z * inner + y

    def to_inner(piece):
        for j in range(1, inner):
            y = ring(j, inner, my_y)
            piece_copy(piece, grp, 2 * chip_of(my_z, y) + core).start()

    def own_outer(i, c):
        z = ring(i, outer, my_z)
        piece_copy(mine + my_slot, grp, 2 * chip_of(z, my_y) + core).start()
        return c

    lax.fori_loop(1, outer, own_outer, 0)
    to_inner(mine + my_slot)
    piece_copy(mine + my_slot, grp, sibling).start()
    piece_copy(theirs + my_slot, grp, sibling).start()

    def send_bias(i, c):
        d = ring(i, n, me)
        pltpu.make_async_remote_copy(
            src_ref=bias.at[my_slot], dst_ref=bias.at[my_slot], send_sem=bs_sem, recv_sem=br_sem,
            device_id=to(d), device_id_type=MESH_ID,
        ).start()
        return c

    lax.fori_loop(1, n, send_bias, 0)

    recv1[me] = send1[me]
    arrived = recv1.at[pl.ds(0, n - 1)]
    pltpu.make_async_copy(arrived, arrived, r1_sem).wait()

    def pairs(s, c):
        v = recv1[s].astype(F32).reshape(al, 8, channels)
        even[s + 8] = v
        for a in range(al):
            odd[s + 8, a, 0:4, :] = v[a, 4:8]
            odd[s + 7, a, 4:8, :] = v[a, 0:4]
        return c

    lax.fori_loop(0, n, pairs, 0)

    def radial_chunk(i, c):
        p = i * 4
        acc = jnp.zeros((4, al, 8, channels), F32)
        for k in range(taps):
            shift = k - half
            if shift % 2 == 0:
                window = even[pl.ds(p + 8 + shift // 2, 4)]
            else:
                window = odd[pl.ds(p + 8 + (shift - 1) // 2, 4)]
            acc = acc + window * rt_ref[k : k + 1, :][None, None]
        acc = acc + cb_ref[...][None, None]
        send2[pl.ds(p, 4)] = acc.reshape(4, al * 8, channels).astype(BF16)
        return c

    lax.fori_loop(0, n // 4, radial_chunk, 0)

    def exchange2(i, c):
        d = ring(i, n, me)
        pltpu.make_async_remote_copy(
            src_ref=send2.at[d], dst_ref=recv2.at[me], send_sem=s2_sem, recv_sem=r2_sem,
            device_id=to(d), device_id_type=MESH_ID,
        ).start()
        return c

    lax.fori_loop(1, n, exchange2, 0)
    recv2[me] = send2[me]

    def from_outer(i, c):
        piece = mine + base + chip_of(ring(i, outer, my_z), my_y)
        piece_copy(piece, grp, sibling).wait_recv()
        to_inner(piece)
        piece_copy(piece, 1 - grp, me).start()
        piece_copy(piece, grp, sibling).start()
        return c

    lax.fori_loop(1, outer, from_outer, 0)

    def from_inner(i, c):
        for j in range(1, inner):
            piece = mine + base + chip_of(ring(i, outer, my_z), ring(j, inner, my_y))
            piece_copy(piece, grp, sibling).wait_recv()
            piece_copy(piece, 1 - grp, me).start()
            piece_copy(piece, grp, sibling).start()
        return c

    lax.fori_loop(0, outer, from_inner, 0)

    def from_group(i, c):
        piece = theirs + base + ring(i, chips, my_chip)
        piece_copy(piece, grp, sibling).wait_recv()
        piece_copy(piece, grp, sibling).start()
        return c

    lax.fori_loop(1, chips, from_group, 0)

    arrived3 = bias.at[pl.ds(0, n - 1)]
    pltpu.make_async_copy(arrived3, arrived3, br_sem).wait()
    arrived2 = recv2.at[pl.ds(0, n - 1)]
    pltpu.make_async_copy(arrived2, arrived2, r2_sem).wait()

    block = min(16, n)
    rows = block * 16

    def norm(b, c):
        v = recv2[pl.ds(b * block, block)].reshape(rows, channels).astype(F32)
        average = jnp.mean(v, axis=-1, keepdims=True)
        centred = v - average
        variance = jnp.mean(centred * centred, axis=-1, keepdims=True)
        z = centred * lax.rsqrt(variance + 1e-06) * lg_ref[...] + lb_ref[...]
        normed[pl.ds(pl.multiple_of(b * rows, rows), rows), :] = z.astype(BF16)
        return c

    lax.fori_loop(0, n // block, norm, 0)

    def flat(w):
        if hl % 16:
            return w.astype(F32).reshape(per * hl, channels).astype(BF16)
        return w.reshape(per * hl, channels)

    def project(z, first):
        w_in = flat(wts[pl.ds(first, per)])
        w_out = flat(wts[pl.ds(n + first, per)])
        b_in = jnp.sum(bias[pl.ds(first, per)], axis=0)
        u = lax.dot_general(z, w_in, (((1,), (1,)), ((), ())), preferred_element_type=F32) + b_in
        g = 0.5 * u * (1.0 + jnp.tanh(0.7978845608028654 * (u + 0.044715 * (u * u * u))))
        return jnp.dot(g.astype(BF16), w_out, preferred_element_type=F32)

    def others(i, c):
        piece_copy(other + i, grp, sibling).wait_recv()
        piece_copy(n + other + i, grp, sibling).wait_recv()
        return c

    def mlp(b, c, late):
        at = pl.ds(pl.multiple_of(b * rows, rows), rows)
        z = normed[at, :]
        total = project(z, base)
        for g in range(1, chips // per):
            total = total + project(z, base + g * per)
        if late:
            lax.fori_loop(0, chips, others, 0)
        for g in range(chips // per):
            total = total + project(z, other + g * per)
        branch = (ls_ref[...] * (total + bo_ref[...])).astype(BF16)
        o_ref[at, :] = (x_ref[at, :].astype(F32) + branch.astype(F32)).astype(BF16)
        return c

    mlp(0, 0, True)
    if n // block > 1:
        lax.fori_loop(1, n // block, lambda b, c: mlp(b, c, False), 0)

    sent = send1.at[pl.ds(0, n - 1)]
    pltpu.make_async_copy(sent, sent, s1_sem).wait()
    sent2 = send2.at[pl.ds(0, n - 1)]
    pltpu.make_async_copy(sent2, sent2, s2_sem).wait()
    passed = wts.at[pl.ds(0, 2 * n - 2)]
    pltpu.make_async_copy(passed, passed, ws_sem).wait()
    pltpu.make_async_copy(arrived3, arrived3, bs_sem).wait()


def local(
    features,
    axial_taps,
    radial_taps,
    conv_bias,
    ln_gain,
    ln_bias,
    w_in,
    b_in,
    w_out,
    b_out,
    layer_scale,
    n,
    groups,
):
    axial, radial, theta, channels = features.shape
    taps = axial_taps.shape[0]
    hl = w_in.shape[0]
    al = axial // n
    inner = 1
    while 4 * inner * inner <= n // 2:
        inner *= 2
    assert groups == 2
    assert radial * theta == 8 and al == 2 and channels == 256 and taps == 31
    flat = features.reshape(axial * 8, channels)

    def row(v):
        return v.reshape(1, -1)

    vmem = pl.BlockSpec(memory_space=pltpu.VMEM)
    dma = pltpu.SemaphoreType.DMA
    out = pl.pallas_call(
        functools.partial(kernel, n, inner, taps, al, hl),
        out_shape=jax.ShapeDtypeStruct(flat.shape, BF16),
        in_specs=[vmem] * 11,
        out_specs=vmem,
        scratch_shapes=[
            pltpu.VMEM((axial + taps - 1, 8, channels), F32),
            pltpu.VMEM((n + 16, al, 8, channels), F32),
            pltpu.VMEM((n + 16, al, 8, channels), F32),
            pltpu.VMEM((n, 16, channels), BF16),
            pltpu.VMEM((n, 16, channels), BF16),
            pltpu.VMEM((n, 16, channels), BF16),
            pltpu.VMEM((n, 16, channels), BF16),
            pltpu.VMEM((2 * n, hl, channels), BF16),
            pltpu.VMEM((n, 1, channels), F32),
            pltpu.VMEM((axial * 8, channels), BF16),
            dma, dma, dma, dma, dma, dma, dma,
            dma((2 * n,)),
        ],
        compiler_params=pltpu.CompilerParams(
            collective_id=0, has_side_effects=True, vmem_limit_bytes=40 * 1024 * 1024
        ),
        cost_estimate=pl.CostEstimate(
            flops=axial * 8 * channels * 4 * (n * hl + taps),
            bytes_accessed=4 * axial * 8 * channels + 4 * n * hl * channels,
            transcendentals=axial * 8 * n * hl,
        ),
    )(
        flat, axial_taps, radial_taps, row(conv_bias), row(ln_gain), row(ln_bias),
        w_in, row(b_in), w_out, row(b_out), row(layer_scale),
    )
    return out.reshape(features.shape)


def solution(mesh):
    in_specs = (
        P("groups", "row", None, None),
        P(),
        P(),
        P(),
        P(),
        P(),
        P("row", None),
        P("row"),
        P("row", None),
        P(),
        P(),
    )
    out_specs = P("groups", "row", None, None)
    body = functools.partial(local, n=mesh.shape["row"], groups=mesh.shape["groups"])
    return jax.shard_map(body, mesh=mesh, in_specs=in_specs, out_specs=out_specs, check_vma=False)
```

```python
import functools

import jax
import jax.numpy as jnp
from jax import lax
from jax.experimental import pallas as pl
from jax.experimental.pallas import tpu as pltpu
from jax.sharding import PartitionSpec as P

MESH_ID = pl.DeviceIdType.MESH
F32 = jnp.float32
BF16 = jnp.bfloat16


def kernel(
    n, inner, taps, al, hl,
    x_ref, at_ref, rt_ref, cb_ref, lg_ref, lb_ref, wi_ref, bi_ref, wo_ref, bo_ref, ls_ref,
    o_ref,
    xpad, even, odd, send1, recv1, send2, recv2, wts, bias, normed,
    s1_sem, r1_sem, s2_sem, r2_sem, ws_sem, bs_sem, br_sem, wr_sem,
):
    channels = x_ref.shape[1]
    axial = x_ref.shape[0] // 8
    half = taps // 2
    per = channels // hl
    chips = n // 2
    me = lax.axis_index("row")
    grp = lax.axis_index("groups")
    core = lax.rem(me, 2)
    my_chip = lax.div(me, 2)
    sibling = me + 1 - 2 * core
    my_slot = core * chips + my_chip
    base = core * chips
    other = (1 - core) * chips
    outer = chips // inner
    my_z = lax.div(my_chip, inner)
    my_y = lax.rem(my_chip, inner)

    def to(d):
        return (grp, d)

    def ring(i, size, start):
        d = start + i
        return jnp.where(d >= size, d - size, d)

    barrier = pltpu.get_barrier_semaphore()

    def greet(i, c):
        pl.semaphore_signal(barrier, inc=1, device_id=to(ring(i, n, me)), device_id_type=MESH_ID)
        return c

    lax.fori_loop(1, n, greet, 0)
    pl.semaphore_signal(barrier, inc=1, device_id=(1 - grp, me), device_id_type=MESH_ID)

    wts[my_slot] = wi_ref[...]
    wts[n + my_slot] = wo_ref[...]
    unit = lax.broadcasted_iota(jnp.int32, (hl, channels), 0)
    lane = lax.broadcasted_iota(jnp.int32, (hl, channels), 1)
    place = (lane == unit + lax.rem(my_slot, per) * hl).astype(F32).astype(BF16)
    bias16 = jnp.broadcast_to(bi_ref[...].astype(F32), (16, hl)).astype(BF16)
    bias[my_slot] = jnp.dot(bias16, place, preferred_element_type=F32)[0:1]

    xpad[0:half] = jnp.zeros((half, 8, channels), F32)
    xpad[axial + half : axial + 2 * half] = jnp.zeros((half, 8, channels), F32)
    zeros8 = jnp.zeros((8, al, 8, channels), F32)
    even[0:8] = zeros8
    even[n + 8 : n + 16] = zeros8
    odd[0:8] = zeros8
    odd[n + 7 : n + 15] = zeros8
    odd[n + 15] = zeros8[0]

    def widen(i, c):
        rows = x_ref[pl.ds(pl.multiple_of(i * 64, 64), 64), :].astype(F32)
        xpad[pl.ds(half + i * 8, 8)] = rows.reshape(8, 8, channels)
        return c

    lax.fori_loop(0, axial // 8, widen, 0)

    def axial_chunk(i, c):
        acc = jnp.zeros((8, 8, channels), F32)
        for k in range(taps):
            acc = acc + xpad[pl.ds(i * 8 + k, 8)] * at_ref[k : k + 1, :][None]
        send1[pl.ds(i * 4, 4)] = acc.reshape(4, 16, channels).astype(BF16)
        return c

    lax.fori_loop(0, axial // 8, axial_chunk, 0)

    pl.semaphore_wait(barrier, n)

    def exchange1(i, c):
        d = ring(i, n, me)
        pltpu.make_async_remote_copy(
            src_ref=send1.at[d], dst_ref=recv1.at[me], send_sem=s1_sem, recv_sem=r1_sem,
            device_id=to(d), device_id_type=MESH_ID,
        ).start()
        return c

    lax.fori_loop(1, n, exchange1, 0)

    mine = grp * n
    theirs = (1 - grp) * n

    def piece_copy(piece, g, d):
        return pltpu.make_async_remote_copy(
            src_ref=wts.at[piece], dst_ref=wts.at[piece], send_sem=ws_sem,
            recv_sem=wr_sem.at[piece], device_id=(g, d), device_id_type=MESH_ID,
        )

    def chip_of(z, y):
        return z * inner + y

    def to_inner(piece):
        for j in range(1, inner):
            y = ring(j, inner, my_y)
            piece_copy(piece, grp, 2 * chip_of(my_z, y) + core).start()

    def own_outer(i, c):
        z = ring(i, outer, my_z)
        piece_copy(mine + my_slot, grp, 2 * chip_of(z, my_y) + core).start()
        return c

    lax.fori_loop(1, outer, own_outer, 0)
    to_inner(mine + my_slot)
    piece_copy(mine + my_slot, grp, sibling).start()
    piece_copy(theirs + my_slot, grp, sibling).start()

    def send_bias(i, c):
        d = ring(i, n, me)
        pltpu.make_async_remote_copy(
            src_ref=bias.at[my_slot], dst_ref=bias.at[my_slot], send_sem=bs_sem, recv_sem=br_sem,
            device_id=to(d), device_id_type=MESH_ID,
        ).start()
        return c

    lax.fori_loop(1, n, send_bias, 0)

    recv1[me] = send1[me]
    arrived = recv1.at[pl.ds(0, n - 1)]
    pltpu.make_async_copy(arrived, arrived, r1_sem).wait()

    def from_outer(i, c):
        piece = mine + base + chip_of(ring(i, outer, my_z), my_y)
        piece_copy(piece, grp, sibling).wait_recv()
        to_inner(piece)
        piece_copy(piece, 1 - grp, me).start()
        piece_copy(piece, grp, sibling).start()
        return c

    lax.fori_loop(1, outer, from_outer, 0)

    def pairs(s, c):
        v = recv1[s].astype(F32).reshape(al, 8, channels)
        even[s + 8] = v
        for a in range(al):
            odd[s + 8, a, 0:4, :] = v[a, 4:8]
            odd[s + 7, a, 4:8, :] = v[a, 0:4]
        return c

    lax.fori_loop(0, n, pairs, 0)

    def radial_chunk(i, c):
        p = i * 4
        acc = jnp.zeros((4, al, 8, channels), F32)
        for k in range(taps):
            shift = k - half
            if shift % 2 == 0:
                window = even[pl.ds(p + 8 + shift // 2, 4)]
            else:
                window = odd[pl.ds(p + 8 + (shift - 1) // 2, 4)]
            acc = acc + window * rt_ref[k : k + 1, :][None, None]
        acc = acc + cb_ref[...][None, None]
        send2[pl.ds(p, 4)] = acc.reshape(4, al * 8, channels).astype(BF16)
        return c

    lax.fori_loop(0, n // 4, radial_chunk, 0)

    def exchange2(i, c):
        d = ring(i, n, me)
        pltpu.make_async_remote_copy(
            src_ref=send2.at[d], dst_ref=recv2.at[me], send_sem=s2_sem, recv_sem=r2_sem,
            device_id=to(d), device_id_type=MESH_ID,
        ).start()
        return c

    lax.fori_loop(1, n, exchange2, 0)
    recv2[me] = send2[me]

    def from_inner(i, c):
        for j in range(1, inner):
            piece = mine + base + chip_of(ring(i, outer, my_z), ring(j, inner, my_y))
            piece_copy(piece, grp, sibling).wait_recv()
            piece_copy(piece, 1 - grp, me).start()
            piece_copy(piece, grp, sibling).start()
        return c

    lax.fori_loop(0, outer, from_inner, 0)

    def from_group(i, c):
        piece = theirs + base + ring(i, chips, my_chip)
        piece_copy(piece, grp, sibling).wait_recv()
        piece_copy(piece, grp, sibling).start()
        return c

    lax.fori_loop(1, chips, from_group, 0)

    arrived3 = bias.at[pl.ds(0, n - 1)]
    pltpu.make_async_copy(arrived3, arrived3, br_sem).wait()
    arrived2 = recv2.at[pl.ds(0, n - 1)]
    pltpu.make_async_copy(arrived2, arrived2, r2_sem).wait()

    block = min(16, n)
    rows = block * 16

    def norm(b, c):
        v = recv2[pl.ds(b * block, block)].reshape(rows, channels).astype(F32)
        average = jnp.mean(v, axis=-1, keepdims=True)
        centred = v - average
        variance = jnp.mean(centred * centred, axis=-1, keepdims=True)
        z = centred * lax.rsqrt(variance + 1e-06) * lg_ref[...] + lb_ref[...]
        normed[pl.ds(pl.multiple_of(b * rows, rows), rows), :] = z.astype(BF16)
        return c

    lax.fori_loop(0, n // block, norm, 0)

    def flat(w):
        if hl % 16:
            return w.astype(F32).reshape(per * hl, channels).astype(BF16)
        return w.reshape(per * hl, channels)

    def project(z, first):
        w_in = flat(wts[pl.ds(first, per)])
        w_out = flat(wts[pl.ds(n + first, per)])
        b_in = jnp.sum(bias[pl.ds(first, per)], axis=0)
        u = lax.dot_general(z, w_in, (((1,), (1,)), ((), ())), preferred_element_type=F32) + b_in
        g = 0.5 * u * (1.0 + jnp.tanh(0.7978845608028654 * (u + 0.044715 * (u * u * u))))
        return jnp.dot(g.astype(BF16), w_out, preferred_element_type=F32)

    def others(i, c):
        piece_copy(other + i, grp, sibling).wait_recv()
        piece_copy(n + other + i, grp, sibling).wait_recv()
        return c

    def mlp(b, c, late):
        at = pl.ds(pl.multiple_of(b * rows, rows), rows)
        z = normed[at, :]
        total = project(z, base)
        for g in range(1, chips // per):
            total = total + project(z, base + g * per)
        if late:
            lax.fori_loop(0, chips, others, 0)
        for g in range(chips // per):
            total = total + project(z, other + g * per)
        branch = (ls_ref[...] * (total + bo_ref[...])).astype(BF16)
        o_ref[at, :] = (x_ref[at, :].astype(F32) + branch.astype(F32)).astype(BF16)
        return c

    mlp(0, 0, True)
    if n // block > 1:
        lax.fori_loop(1, n // block, lambda b, c: mlp(b, c, False), 0)

    sent = send1.at[pl.ds(0, n - 1)]
    pltpu.make_async_copy(sent, sent, s1_sem).wait()
    sent2 = send2.at[pl.ds(0, n - 1)]
    pltpu.make_async_copy(sent2, sent2, s2_sem).wait()
    passed = wts.at[pl.ds(0, 2 * n - 2)]
    pltpu.make_async_copy(passed, passed, ws_sem).wait()
    pltpu.make_async_copy(arrived3, arrived3, bs_sem).wait()


def local(
    features,
    axial_taps,
    radial_taps,
    conv_bias,
    ln_gain,
    ln_bias,
    w_in,
    b_in,
    w_out,
    b_out,
    layer_scale,
    n,
    groups,
):
    axial, radial, theta, channels = features.shape
    taps = axial_taps.shape[0]
    hl = w_in.shape[0]
    al = axial // n
    inner = 1
    while 4 * inner * inner <= n // 2:
        inner *= 2
    assert groups == 2
    assert radial * theta == 8 and al == 2 and channels == 256 and taps == 31
    flat = features.reshape(axial * 8, channels)

    def row(v):
        return v.reshape(1, -1)

    vmem = pl.BlockSpec(memory_space=pltpu.VMEM)
    dma = pltpu.SemaphoreType.DMA
    out = pl.pallas_call(
        functools.partial(kernel, n, inner, taps, al, hl),
        out_shape=jax.ShapeDtypeStruct(flat.shape, BF16),
        in_specs=[vmem] * 11,
        out_specs=vmem,
        scratch_shapes=[
            pltpu.VMEM((axial + taps - 1, 8, channels), F32),
            pltpu.VMEM((n + 16, al, 8, channels), F32),
            pltpu.VMEM((n + 16, al, 8, channels), F32),
            pltpu.VMEM((n, 16, channels), BF16),
            pltpu.VMEM((n, 16, channels), BF16),
            pltpu.VMEM((n, 16, channels), BF16),
            pltpu.VMEM((n, 16, channels), BF16),
            pltpu.VMEM((2 * n, hl, channels), BF16),
            pltpu.VMEM((n, 1, channels), F32),
            pltpu.VMEM((axial * 8, channels), BF16),
            dma, dma, dma, dma, dma, dma, dma,
            dma((2 * n,)),
        ],
        compiler_params=pltpu.CompilerParams(
            collective_id=0, has_side_effects=True, vmem_limit_bytes=40 * 1024 * 1024
        ),
        cost_estimate=pl.CostEstimate(
            flops=axial * 8 * channels * 4 * (n * hl + taps),
            bytes_accessed=4 * axial * 8 * channels + 4 * n * hl * channels,
            transcendentals=axial * 8 * n * hl,
        ),
    )(
        flat, axial_taps, radial_taps, row(conv_bias), row(ln_gain), row(ln_bias),
        w_in, row(b_in), w_out, row(b_out), row(layer_scale),
    )
    return out.reshape(features.shape)


def solution(mesh):
    in_specs = (
        P("groups", "row", None, None),
        P(),
        P(),
        P(),
        P(),
        P(),
        P("row", None),
        P("row"),
        P("row", None),
        P(),
        P(),
    )
    out_specs = P("groups", "row", None, None)
    body = functools.partial(local, n=mesh.shape["row"], groups=mesh.shape["groups"])
    return jax.shard_map(body, mesh=mesh, in_specs=in_specs, out_specs=out_specs, check_vma=False)
```

```python
import functools

import jax
import jax.numpy as jnp
from jax import lax
from jax.experimental import pallas as pl
from jax.experimental.pallas import tpu as pltpu
from jax.sharding import PartitionSpec as P

MESH_ID = pl.DeviceIdType.MESH
F32 = jnp.float32
BF16 = jnp.bfloat16


def kernel(
    n, inner, taps, al, hl,
    x_ref, at_ref, rt_ref, cb_ref, lg_ref, lb_ref, wi_ref, bi_ref, wo_ref, bo_ref, ls_ref,
    o_ref,
    xpad, even, odd, send1, recv1, send2, recv2, wts, bias, normed,
    s1_sem, r1_sem, s2_sem, r2_sem, ws_sem, bs_sem, br_sem, wr_sem,
):
    channels = x_ref.shape[1]
    axial = x_ref.shape[0] // 8
    half = taps // 2
    per = channels // hl
    chips = n // 2
    me = lax.axis_index("row")
    grp = lax.axis_index("groups")
    core = lax.rem(me, 2)
    my_chip = lax.div(me, 2)
    sibling = me + 1 - 2 * core
    my_slot = core * chips + my_chip
    base = core * chips
    other = (1 - core) * chips
    outer = chips // inner
    my_z = lax.div(my_chip, inner)
    my_y = lax.rem(my_chip, inner)

    def to(d):
        return (grp, d)

    def ring(i, size, start):
        d = start + i
        return jnp.where(d >= size, d - size, d)

    barrier = pltpu.get_barrier_semaphore()

    def greet(i, c):
        pl.semaphore_signal(barrier, inc=1, device_id=to(ring(i, n, me)), device_id_type=MESH_ID)
        return c

    lax.fori_loop(1, n, greet, 0)
    pl.semaphore_signal(barrier, inc=1, device_id=(1 - grp, me), device_id_type=MESH_ID)

    wts[my_slot] = wi_ref[...]
    wts[n + my_slot] = wo_ref[...]
    unit = lax.broadcasted_iota(jnp.int32, (hl, channels), 0)
    lane = lax.broadcasted_iota(jnp.int32, (hl, channels), 1)
    place = (lane == unit + lax.rem(my_slot, per) * hl).astype(F32).astype(BF16)
    bias16 = jnp.broadcast_to(bi_ref[...].astype(F32), (16, hl)).astype(BF16)
    bias[my_slot] = jnp.dot(bias16, place, preferred_element_type=F32)[0:1]

    xpad[0:half] = jnp.zeros((half, 8, channels), F32)
    xpad[axial + half : axial + 2 * half] = jnp.zeros((half, 8, channels), F32)
    zeros8 = jnp.zeros((8, al, 8, channels), F32)
    even[0:8] = zeros8
    even[n + 8 : n + 16] = zeros8
    odd[0:8] = zeros8
    odd[n + 7 : n + 15] = zeros8
    odd[n + 15] = zeros8[0]

    def widen(i, c):
        rows = x_ref[pl.ds(pl.multiple_of(i * 64, 64), 64), :].astype(F32)
        xpad[pl.ds(half + i * 8, 8)] = rows.reshape(8, 8, channels)
        return c

    lax.fori_loop(0, axial // 8, widen, 0)

    def axial_chunk(i, c):
        acc = jnp.zeros((8, 8, channels), F32)
        for k in range(taps):
            acc = acc + xpad[pl.ds(i * 8 + k, 8)] * at_ref[k : k + 1, :][None]
        send1[pl.ds(i * 4, 4)] = acc.reshape(4, 16, channels).astype(BF16)
        return c

    lax.fori_loop(0, axial // 8, axial_chunk, 0)

    pl.semaphore_wait(barrier, n)

    def exchange1(i, c):
        d = ring(i, n, me)
        pltpu.make_async_remote_copy(
            src_ref=send1.at[d], dst_ref=recv1.at[me], send_sem=s1_sem, recv_sem=r1_sem,
            device_id=to(d), device_id_type=MESH_ID,
        ).start()
        return c

    lax.fori_loop(1, n, exchange1, 0)

    mine = grp * n
    theirs = (1 - grp) * n

    def piece_copy(piece, g, d):
        return pltpu.make_async_remote_copy(
            src_ref=wts.at[piece], dst_ref=wts.at[piece], send_sem=ws_sem,
            recv_sem=wr_sem.at[piece], device_id=(g, d), device_id_type=MESH_ID,
        )

    def chip_of(z, y):
        return z * inner + y

    def to_inner(piece):
        for j in range(1, inner):
            y = ring(j, inner, my_y)
            piece_copy(piece, grp, 2 * chip_of(my_z, y) + core).start()

    def own_outer(i, c):
        z = ring(i, outer, my_z)
        piece_copy(mine + my_slot, grp, 2 * chip_of(z, my_y) + core).start()
        return c

    lax.fori_loop(1, outer, own_outer, 0)
    to_inner(mine + my_slot)
    to_inner(theirs + my_slot)
    piece_copy(mine + my_slot, grp, sibling).start()
    piece_copy(theirs + my_slot, grp, sibling).start()

    def send_bias(i, c):
        d = ring(i, n, me)
        pltpu.make_async_remote_copy(
            src_ref=bias.at[my_slot], dst_ref=bias.at[my_slot], send_sem=bs_sem, recv_sem=br_sem,
            device_id=to(d), device_id_type=MESH_ID,
        ).start()
        return c

    lax.fori_loop(1, n, send_bias, 0)

    recv1[me] = send1[me]
    arrived = recv1.at[pl.ds(0, n - 1)]
    pltpu.make_async_copy(arrived, arrived, r1_sem).wait()

    def from_outer(i, c):
        piece = mine + base + chip_of(ring(i, outer, my_z), my_y)
        piece_copy(piece, grp, sibling).wait_recv()
        to_inner(piece)
        piece_copy(piece, 1 - grp, me).start()
        piece_copy(piece, grp, sibling).start()
        return c

    lax.fori_loop(1, outer, from_outer, 0)

    def from_inner(i, c, swap=True):
        for j in range(1, inner):
            piece = mine + base + chip_of(ring(i, outer, my_z), ring(j, inner, my_y))
            piece_copy(piece, grp, sibling).wait_recv()
            if swap:
                piece_copy(piece, 1 - grp, me).start()
            piece_copy(piece, grp, sibling).start()
        return c

    from_inner(0, 0, swap=False)

    def pairs(s, c):
        v = recv1[s].astype(F32).reshape(al, 8, channels)
        even[s + 8] = v
        for a in range(al):
            odd[s + 8, a, 0:4, :] = v[a, 4:8]
            odd[s + 7, a, 4:8, :] = v[a, 0:4]
        return c

    lax.fori_loop(0, n, pairs, 0)

    def radial_chunk(i, c):
        p = i * 4
        acc = jnp.zeros((4, al, 8, channels), F32)
        for k in range(taps):
            shift = k - half
            if shift % 2 == 0:
                window = even[pl.ds(p + 8 + shift // 2, 4)]
            else:
                window = odd[pl.ds(p + 8 + (shift - 1) // 2, 4)]
            acc = acc + window * rt_ref[k : k + 1, :][None, None]
        acc = acc + cb_ref[...][None, None]
        send2[pl.ds(p, 4)] = acc.reshape(4, al * 8, channels).astype(BF16)
        return c

    lax.fori_loop(0, n // 4, radial_chunk, 0)

    def exchange2(i, c):
        d = ring(i, n, me)
        pltpu.make_async_remote_copy(
            src_ref=send2.at[d], dst_ref=recv2.at[me], send_sem=s2_sem, recv_sem=r2_sem,
            device_id=to(d), device_id_type=MESH_ID,
        ).start()
        return c

    lax.fori_loop(1, n, exchange2, 0)
    recv2[me] = send2[me]

    lax.fori_loop(1, outer, from_inner, 0)

    def from_group(i, c):
        piece = theirs + base + ring(i, chips, my_chip)
        piece_copy(piece, grp, sibling).wait_recv()
        piece_copy(piece, grp, sibling).start()
        return c


    arrived3 = bias.at[pl.ds(0, n - 1)]
    pltpu.make_async_copy(arrived3, arrived3, br_sem).wait()
    arrived2 = recv2.at[pl.ds(0, n - 1)]
    pltpu.make_async_copy(arrived2, arrived2, r2_sem).wait()

    block = min(16, n)
    rows = block * 16

    def norm(b, c):
        v = recv2[pl.ds(b * block, block)].reshape(rows, channels).astype(F32)
        average = jnp.mean(v, axis=-1, keepdims=True)
        centred = v - average
        variance = jnp.mean(centred * centred, axis=-1, keepdims=True)
        z = centred * lax.rsqrt(variance + 1e-06) * lg_ref[...] + lb_ref[...]
        normed[pl.ds(pl.multiple_of(b * rows, rows), rows), :] = z.astype(BF16)
        return c

    lax.fori_loop(0, n // block, norm, 0)

    def flat(w):
        if hl % 16:
            return w.astype(F32).reshape(per * hl, channels).astype(BF16)
        return w.reshape(per * hl, channels)

    def project(z, first):
        w_in = flat(wts[pl.ds(first, per)])
        w_out = flat(wts[pl.ds(n + first, per)])
        b_in = jnp.sum(bias[pl.ds(first, per)], axis=0)
        u = lax.dot_general(z, w_in, (((1,), (1,)), ((), ())), preferred_element_type=F32) + b_in
        g = 0.5 * u * (1.0 + jnp.tanh(0.7978845608028654 * (u + 0.044715 * (u * u * u))))
        return jnp.dot(g.astype(BF16), w_out, preferred_element_type=F32)

    def others(i, c):
        piece_copy(other + i, grp, sibling).wait_recv()
        piece_copy(n + other + i, grp, sibling).wait_recv()
        return c

    def mlp(b, c, late):
        at = pl.ds(pl.multiple_of(b * rows, rows), rows)
        z = normed[at, :]
        total = project(z, base)
        for g in range(1, chips // per):
            total = total + project(z, base + g * per)
        if late:
            lax.fori_loop(0, chips, others, 0)
        for g in range(chips // per):
            total = total + project(z, other + g * per)
        branch = (ls_ref[...] * (total + bo_ref[...])).astype(BF16)
        o_ref[at, :] = (x_ref[at, :].astype(F32) + branch.astype(F32)).astype(BF16)
        return c

    lax.fori_loop(1, chips, from_group, 0)
    mlp(0, 0, True)
    if n // block > 1:
        lax.fori_loop(1, n // block, lambda b, c: mlp(b, c, False), 0)

    sent = send1.at[pl.ds(0, n - 1)]
    pltpu.make_async_copy(sent, sent, s1_sem).wait()
    sent2 = send2.at[pl.ds(0, n - 1)]
    pltpu.make_async_copy(sent2, sent2, s2_sem).wait()
    passed = wts.at[pl.ds(0, 2 * n - 2)]
    pltpu.make_async_copy(passed, passed, ws_sem).wait()
    pltpu.make_async_copy(arrived3, arrived3, bs_sem).wait()


def local(
    features,
    axial_taps,
    radial_taps,
    conv_bias,
    ln_gain,
    ln_bias,
    w_in,
    b_in,
    w_out,
    b_out,
    layer_scale,
    n,
    groups,
):
    axial, radial, theta, channels = features.shape
    taps = axial_taps.shape[0]
    hl = w_in.shape[0]
    al = axial // n
    inner = 1
    while 4 * inner * inner <= n // 2:
        inner *= 2
    assert groups == 2
    assert radial * theta == 8 and al == 2 and channels == 256 and taps == 31
    flat = features.reshape(axial * 8, channels)

    def row(v):
        return v.reshape(1, -1)

    vmem = pl.BlockSpec(memory_space=pltpu.VMEM)
    dma = pltpu.SemaphoreType.DMA
    out = pl.pallas_call(
        functools.partial(kernel, n, inner, taps, al, hl),
        out_shape=jax.ShapeDtypeStruct(flat.shape, BF16),
        in_specs=[vmem] * 11,
        out_specs=vmem,
        scratch_shapes=[
            pltpu.VMEM((axial + taps - 1, 8, channels), F32),
            pltpu.VMEM((n + 16, al, 8, channels), F32),
            pltpu.VMEM((n + 16, al, 8, channels), F32),
            pltpu.VMEM((n, 16, channels), BF16),
            pltpu.VMEM((n, 16, channels), BF16),
            pltpu.VMEM((n, 16, channels), BF16),
            pltpu.VMEM((n, 16, channels), BF16),
            pltpu.VMEM((2 * n, hl, channels), BF16),
            pltpu.VMEM((n, 1, channels), F32),
            pltpu.VMEM((axial * 8, channels), BF16),
            dma, dma, dma, dma, dma, dma, dma,
            dma((2 * n,)),
        ],
        compiler_params=pltpu.CompilerParams(
            collective_id=0, has_side_effects=True, vmem_limit_bytes=40 * 1024 * 1024
        ),
        cost_estimate=pl.CostEstimate(
            flops=axial * 8 * channels * 4 * (n * hl + taps),
            bytes_accessed=4 * axial * 8 * channels + 4 * n * hl * channels,
            transcendentals=axial * 8 * n * hl,
        ),
    )(
        flat, axial_taps, radial_taps, row(conv_bias), row(ln_gain), row(ln_bias),
        w_in, row(b_in), w_out, row(b_out), row(layer_scale),
    )
    return out.reshape(features.shape)


def solution(mesh):
    in_specs = (
        P("groups", "row", None, None),
        P(),
        P(),
        P(),
        P(),
        P(),
        P("row", None),
        P("row"),
        P("row", None),
        P(),
        P(),
    )
    out_specs = P("groups", "row", None, None)
    body = functools.partial(local, n=mesh.shape["row"], groups=mesh.shape["groups"])
    return jax.shard_map(body, mesh=mesh, in_specs=in_specs, out_specs=out_specs, check_vma=False)
```
